32 devices in a mesh: grp: 4 (over x, core), sub: 8 (over z, y).
Axes of the slice: x: 2, y: 2, z: 4, core: 2. Of those that a mesh axis runs over, the one named last changes fastest.
Arguments:
- operators: float32 [4, 8, 4, 512, 512], P('grp', 'sub'), may hold values from -1 to 6
- counts: int32 [4, 8], P('grp', 'sub'), may hold values from 1 to 4, as said below
- pair_rows: int32 [4, 8, 4, 256], P('grp', 'sub'), may hold values from -256 to 256, as said below
- gap: float32 [4, 8, 4, 256, 128], P('grp', 'sub'), may hold values from -6 to 6
Outputs:
- multipliers: float32 [4, 8, 4, 256, 128], P('grp', 'sub')
- residual: float32 [4, 8, 4, 256, 128], P('grp', 'sub')
The draws below stay inside these ranges and needn't reach their ends.
Inputs may be any that keep to these rules, and one draw needn't show every extreme that they name: `counts`: each group has at least one owner with 4 subdomains. `pair_rows`: for each group, owner and slot the absolute values are a permutation of 1 to 256.
All inputs are finite; a program needn't handle non-finite values.
Results may differ from the reference program's by a relative error of at most 0.00022.
Values sent between devices are 32-bit elements; how exact they have to be, the bound alone decides.
No kernel may reach another device: no remote copies, remote signals or barrier semaphores. Data moves between devices by JAX's collectives and lax.ppermute only.
A program may use at most 64 MiB of HBM per device.

```python
import math
import jax
import jax.numpy as jnp
from jax import lax

M = 512
H = 256
RHS = 128
SLOTS = 4
ITERS = 6
GROUPS = 4
OWNERS = 8


def draw_operators(key, part):
    k_diag, k_noise = jax.random.split(jax.random.fold_in(key, 11))
    shape = (GROUPS, OWNERS, SLOTS, M, M)
    noise = jnp.clip(jax.random.normal(k_noise, shape, jnp.float32), -4.0, 4.0)
    noise = noise * (0.75 / math.sqrt(M))
    symmetric = (noise + jnp.swapaxes(noise, 3, 4)) * (1.0 / math.sqrt(2.0))
    diagonal = jax.random.uniform(k_diag, (GROUPS, OWNERS, SLOTS, M), jnp.float32, 2.0, 5.5)
    identity = jnp.eye(M, dtype=jnp.float32)
    return symmetric * (1.0 - identity) + diagonal[..., None] * identity


def draw_counts(key, part):
    k_first, k_second = jax.random.split(jax.random.fold_in(key, 23))
    levels = jax.random.randint(k_first, (GROUPS, OWNERS), 0, 10)
    tally = 1 + (levels >= 6).astype(jnp.int32) + (levels >= 8).astype(jnp.int32) + (levels >= 9).astype(jnp.int32)
    chosen = jax.random.randint(k_second, (GROUPS,), 0, OWNERS)
    busiest = jnp.arange(OWNERS, dtype=jnp.int32)[None, :] == chosen[:, None]
    return jnp.where(busiest, SLOTS, tally).astype(jnp.int32)


def draw_pair_rows(key, part):
    k_first, k_second = jax.random.split(jax.random.fold_in(key, 37))
    shape = (GROUPS, OWNERS, SLOTS, H)
    scores = jax.random.randint(k_first, shape, 0, 1048576) * H + jnp.arange(H, dtype=jnp.int32)
    ordering = jnp.argsort(scores, axis=-1).astype(jnp.int32)
    flips = 2 * jax.random.randint(k_second, shape, 0, 2) - 1
    return ((ordering + 1) * flips).astype(jnp.int32)


def shard_levels(own_key, shape, cuts, least, largest):
    def one(axis_at, parts):
        steps = jax.random.uniform(jax.random.fold_in(jax.random.fold_in(own_key, 6), axis_at), (parts,), jnp.float32, least / len(cuts), largest / len(cuts))
        return jnp.repeat(jnp.exp(steps), shape[axis_at] // parts).reshape((-1,) + (1,) * (len(shape) - axis_at - 1))

    level = one(*cuts[0])
    for cut in cuts[1:]:
        level = level * one(*cut)
    return level


def gaussian(key, shape, deviation, most, shards=(), held_as=jnp.bfloat16):
    values = jax.random.normal(key, shape, jnp.float32) * deviation
    if len(shards) > 0:
        values = shard_levels(key, shape, shards, -0.22, 0.18) * values
    return jnp.clip(values, min=-most, max=most).astype(held_as)


def setup_inputs(seed: int = 0) -> dict:
    keys = jax.random.split(jax.random.key(seed), 5)
    operators = draw_operators(jax.random.fold_in(keys[4], 71), 0)
    counts = draw_counts(jax.random.fold_in(keys[4], 71), 0)
    pair_rows = draw_pair_rows(jax.random.fold_in(keys[4], 71), 0)
    gap = gaussian(keys[3], (GROUPS, OWNERS, SLOTS, H, RHS), 1.0, 6.0, ((0, 4), (1, 8)), jnp.float32)
    return {"operators": operators, "counts": counts, "pair_rows": pair_rows, "gap": gap}


LOWER = 1.0
UPPER = 14.0


def pick_rows(matrix, picks):
    return matrix[picks]


def place_rows(picks, values):
    return jnp.zeros_like(values).at[picks].set(values)


def reference(operators, counts, pair_rows, gap):
    slot_ids = jnp.arange(SLOTS, dtype=jnp.int32)
    owner_ids = jnp.arange(OWNERS, dtype=jnp.int32)
    occupied = slot_ids[None, None, :] < counts[:, :, None]
    final_slot = slot_ids[None, None, :] == counts[:, :, None] - 1
    exists = occupied & jnp.logical_not((owner_ids[None, :, None] == OWNERS - 1) & final_slot)
    live_mask = occupied.astype(jnp.float32)[..., None, None]
    exist_mask = exists.astype(jnp.float32)[..., None, None]
    top_mask = final_slot[..., None, None]
    top_weight = top_mask.astype(jnp.float32)
    row_index = (jnp.abs(pair_rows) - 1).astype(jnp.int32)
    sign_flip = jnp.sign(pair_rows).astype(jnp.float32)[..., None]
    picker = jax.vmap(jax.vmap(jax.vmap(pick_rows)))
    placer = jax.vmap(jax.vmap(jax.vmap(place_rows)))

    def apply_dual(direction):
        final_block = jnp.sum(direction * top_weight, axis=2)
        from_before = jnp.concatenate([jnp.zeros_like(final_block[:, :1]), final_block[:, :-1]], axis=1)
        previous = jnp.concatenate([from_before[:, :, None], direction[:, :, :-1]], axis=2)
        left_rows = -sign_flip * picker(previous, row_index)
        expanded = jnp.concatenate([left_rows, direction], axis=3) * live_mask
        images = jnp.einsum("gsjmn,gsjnr->gsjmr", operators, expanded, precision=lax.Precision.HIGHEST)
        returned = placer(row_index, -sign_flip * images[:, :, :, :H])
        behind = jnp.concatenate([returned[:, 1:, 0], jnp.zeros_like(returned[:, :1, 0])], axis=1)
        back_next = jnp.concatenate([returned[:, :, 1:], jnp.zeros_like(returned[:, :, :1])], axis=2)
        following = jnp.where(top_mask, behind[:, :, None], back_next)
        return (images[:, :, :, H:] + following) * exist_mask

    centre = (UPPER + LOWER) / 2.0
    radius = (UPPER - LOWER) / 2.0
    spread_ratio = centre / radius
    rho_prev = 1.0 / spread_ratio
    residual = gap * exist_mask
    iterate = jnp.zeros_like(residual)
    direction = residual / centre
    for sweep_num in range(ITERS):
        iterate = iterate + direction
        residual = residual - apply_dual(direction)
        if sweep_num < ITERS - 1:
            rho_next = 1.0 / (2.0 * spread_ratio - rho_prev)
            direction = rho_next * rho_prev * direction + (2.0 * rho_next / radius) * residual
            rho_prev = rho_next
    return iterate, residual
```

```python
import functools

import jax
import jax.numpy as jnp
from jax import lax
from jax.experimental import pallas as pl
from jax.experimental.pallas import tpu as pltpu
from jax.sharding import PartitionSpec as P

ITERS = 6
LOWER = 1.0
UPPER = 14.0
CENTRE = (UPPER + LOWER) / 2.0
RADIUS = (UPPER - LOWER) / 2.0
BF16 = jnp.bfloat16
F32 = jnp.float32
VMEM_BYTES = 24 * 1024 * 1024


def chebyshev_factors():
    spread = CENTRE / RADIUS
    rho = 1.0 / spread
    factors = []
    for _ in range(ITERS - 1):
        rho_new = 1.0 / (2.0 * spread - rho)
        factors.append((rho_new * rho, 2.0 * rho_new / RADIUS))
        rho = rho_new
    return factors


def pairings(groups, owners):
    found = []
    for first in (0, 1):
        route = []
        for g in range(groups):
            for s in range(owners):
                t = s + 1 if (s - first) % 2 == 0 else s - 1
                h = g
                if t < 0 or t >= owners:
                    t = s
                    h = g ^ 1
                if h < groups:
                    route.append((g * owners + s, h * owners + t))
        found.append(route)
    return found


def halves(x):
    high = x.astype(BF16)
    return high, (x - high.astype(F32)).astype(BF16)


def beside(x):
    both = jnp.concatenate(halves(x), axis=1)
    return jnp.concatenate([both, both], axis=0)


def split_dot(matrix, cases):
    wide = jnp.dot(matrix, cases, preferred_element_type=F32)
    width = wide.shape[1] // 2
    return wide[:, :width] + wide[:, width:]


def dot_nt(a, b):
    return lax.dot_general(a, b, (((1,), (1,)), ((), ())), preferred_element_type=F32)


def signed_placement(pairs):
    h = pairs.shape[1]
    rows = lax.broadcasted_iota(jnp.int32, (h, h), 0)
    picked = jnp.abs(pairs) - 1
    sign = jnp.where(pairs > 0, 1.0, -1.0)
    return jnp.where(rows == picked, sign, 0.0).astype(BF16)


def exists_of(count, pos, owners, slot):
    there = jnp.logical_and(slot < count, jnp.logical_or(pos < owners - 1, slot != count - 1))
    return jnp.where(there, 1.0, 0.0)


def first_kernel(owners, info, operators, pairs, gap, left_out, image_out, even_out, odd_out, direction, top, sem):
    count, pos = info[0], info[1]
    slots, h = gap.shape[0], gap.shape[1]
    copy = pltpu.make_async_copy(operators.at[0, 0, 0, pl.ds(0, h)], top, sem)
    copy.start()
    for j in range(slots):
        image_out[j] = gap[j] * exists_of(count, pos, owners, j)
        direction[j] = image_out[j] / CENTRE
    place = signed_placement(pairs[pl.ds(0, 1), :])
    copy.wait()
    high, low = halves(top[...])
    placed = [jnp.dot(place, part, preferred_element_type=F32).astype(BF16) for part in (high, low)]
    square = [dot_nt(part[:, :h], place) for part in placed]
    left_out[...] = square[0] + square[1]
    across = jnp.concatenate([-part[:, h:] for part in placed], axis=1)
    behind = split_dot(across, beside(direction[0]))
    send(pos, direction[count - 1], behind, even_out, odd_out)


def send(pos, ahead, behind, even_out, odd_out):
    is_even = lax.rem(pos, 2) == 0

    @pl.when(is_even)
    def _():
        even_out[...] = ahead
        odd_out[...] = behind

    @pl.when(jnp.logical_not(is_even))
    def _():
        even_out[...] = behind
        odd_out[...] = ahead


def operator_kernel(info, operators, pairs, own_out, lower_out, upper_out, whole, sems):
    count = info[0]
    slots, h = pairs.shape
    copies = [pltpu.make_async_copy(operators.at[0, 0, j], whole.at[j], sems.at[j]) for j in range(slots)]
    for copy in copies:
        copy.start()
    for j in range(slots):
        copies[j].wait()
        place = signed_placement(pairs[pl.ds(j, 1), :])
        squares = []
        for k, part in enumerate(halves(whole[j])):
            columns = pl.ds(k * h, h)
            placed = jnp.dot(place, part[:h], preferred_element_type=F32).astype(BF16)
            upper_out[j, :, columns] = -placed[:, h:]
            turned = dot_nt(jnp.concatenate([placed[:, :h], part[h:, :h]], axis=0), place)
            squares.append(turned[:h])
            lower_out[j, :, columns] = -turned[h:].astype(BF16)
        if j > 0:
            added = jnp.where(j < count, squares[0] + squares[1], 0.0)
            high, low = halves(whole[j - 1, pl.ds(h, h), pl.ds(h, h)] + added)
            own_out[j - 1, :, pl.ds(0, h)] = high
            own_out[j - 1, :, pl.ds(h, h)] = low
    high, low = halves(whole[slots - 1, pl.ds(h, h), pl.ds(h, h)])
    own_out[slots - 1, :, pl.ds(0, h)] = high
    own_out[slots - 1, :, pl.ds(h, h)] = low


def join_kernel(info, own, left, own_out):
    last = info[0] - 1
    h = left.shape[0]
    total = own[last, :, pl.ds(0, h)].astype(F32) + own[last, :, pl.ds(h, h)].astype(F32) + left[...]
    high, low = halves(total)
    own_out[last, :, pl.ds(0, h)] = high
    own_out[last, :, pl.ds(h, h)] = low


def inner_kernel(owners, started, info, own, lower, upper, direction, residual, total, residual_out, total_out):
    count, pos = info[0], info[1]
    slots = direction.shape[0]
    cases = [beside(direction[j]) for j in range(slots)]
    for j in range(slots):
        image = split_dot(own[j], cases[j])
        if j > 0:
            image += split_dot(lower[j], cases[j - 1])
        if j + 1 < slots:
            image += split_dot(upper[j + 1], cases[j + 1])
        residual_out[j] = residual[j] - image * exists_of(count, pos, owners, j)
        total_out[j] = total[j] + direction[j] if started else direction[j]


def received(pos, even_in, odd_in):
    is_even = lax.rem(pos, 2) == 0
    before = jnp.where(is_even, odd_in[...], even_in[...])
    behind = jnp.where(is_even, even_in[...], odd_in[...])
    return jnp.where(pos > 0, before, 0.0), behind


def finish_residual(owners, info, lower, even_in, odd_in, residual, residual_out):
    count, pos = info[0], info[1]
    slots = residual.shape[0]
    before, behind = received(pos, even_in, odd_in)
    for j in range(slots):
        residual_out[j] = residual[j]
    residual_out[0] -= split_dot(lower[0], beside(before)) * exists_of(count, pos, owners, 0)
    last = count - 1
    residual_out[last] -= behind * exists_of(count, pos, owners, last)


def edge_kernel(owners, factors, info, lower, upper, even_in, odd_in, direction, residual, residual_out, direction_out, even_out, odd_out):
    count, pos = info[0], info[1]
    finish_residual(owners, info, lower, even_in, odd_in, residual, residual_out)
    for j in range(direction.shape[0]):
        direction_out[j] = factors[0] * direction[j] + factors[1] * residual_out[j]
    behind = split_dot(upper[0], beside(direction_out[0]))
    send(pos, direction_out[count - 1], behind, even_out, odd_out)


def last_kernel(owners, info, lower, even_in, odd_in, residual, residual_out):
    finish_residual(owners, info, lower, even_in, odd_in, residual, residual_out)


SMEM = pl.BlockSpec(memory_space=pltpu.SMEM)
VMEM = pl.BlockSpec(memory_space=pltpu.VMEM)
ANY = pl.BlockSpec(memory_space=pl.ANY)


def call(kernel, ins, outs, name, scratch=(), aliases=None, flops=0):
    return pl.pallas_call(
        kernel,
        in_specs=ins,
        out_specs=[VMEM] * len(outs),
        out_shape=[jax.ShapeDtypeStruct(shape, kind) for shape, kind in outs],
        scratch_shapes=list(scratch),
        input_output_aliases=aliases or {},
        compiler_params=pltpu.CompilerParams(vmem_limit_bytes=VMEM_BYTES),
        cost_estimate=pl.CostEstimate(flops=flops, bytes_accessed=1000000, transcendentals=0),
        name=name,
    )


def shards(groups, owners, operators, counts, pair_rows, gap):
    pairs, source = pair_rows[0, 0], gap[0, 0]
    slots, h, cases = source.shape
    m = operators.shape[-1]
    pos = lax.axis_index("sub").astype(jnp.int32)
    info = jnp.stack([counts[0, 0], pos])
    evens, odds = pairings(groups, owners)
    ring = [((s + 1) % owners, s) for s in range(owners)]
    field = ((slots, h, cases), F32)
    block = ((h, cases), F32)
    matrices = ((slots, h, 2 * h), BF16)

    def exchange(even, odd):
        odd = lax.ppermute(odd, ("grp", "sub"), odds)
        even = lax.ppermute(even, ("grp", "sub"), evens)
        return even, odd

    left, residual, even, odd, direction = call(
        functools.partial(first_kernel, owners),
        [SMEM, ANY, VMEM, VMEM],
        [((h, h), F32), field, block, block, field],
        "first_messages",
        [pltpu.VMEM((h, m), F32), pltpu.SemaphoreType.DMA],
    )(info, operators, pairs, source)
    even, odd = exchange(even, odd)
    left = lax.ppermute(left, "sub", ring)
    own, lower, upper = call(
        operator_kernel,
        [SMEM, ANY, VMEM],
        [matrices] * 3,
        "block_operators",
        [pltpu.VMEM((slots, m, m), F32), pltpu.SemaphoreType.DMA((slots,))],
    )(info, operators, pairs)
    (own,) = call(join_kernel, [SMEM, VMEM, VMEM], [matrices], "join_left", aliases={1: 0})(info, own, left)
    total = direction
    for step, factors in enumerate(chebyshev_factors() + [None]):
        residual, total = call(
            functools.partial(inner_kernel, owners, step > 0),
            [SMEM] + [VMEM] * 6,
            [field, field],
            "inner_blocks",
            flops=20 * h * h * cases * 4,
        )(info, own, lower, upper, direction, residual, total)
        if factors is None:
            (residual,) = call(
                functools.partial(last_kernel, owners), [SMEM] + [VMEM] * 4, [field], "last_residual"
            )(info, lower, even, odd, residual)
        else:
            residual, direction, even, odd = call(
                functools.partial(edge_kernel, owners, factors),
                [SMEM] + [VMEM] * 6,
                [field, field, block, block],
                "edge_blocks",
            )(info, lower, upper, even, odd, direction, residual)
            even, odd = exchange(even, odd)
    return total[None, None], residual[None, None]


def solution(mesh):
    groups, owners = mesh.shape["grp"], mesh.shape["sub"]
    return jax.shard_map(
        functools.partial(shards, groups, owners),
        mesh=mesh,
        in_specs=(
            P("grp", "sub", None, None, None),
            P("grp", "sub"),
            P("grp", "sub", None, None),
            P("grp", "sub", None, None, None),
        ),
        out_specs=(P("grp", "sub", None, None, None), P("grp", "sub", None, None, None)),
        check_vma=False,
    )
```

```python
import functools

import jax
import jax.numpy as jnp
from jax import lax
from jax.experimental import pallas as pl
from jax.experimental.pallas import tpu as pltpu
from jax.sharding import PartitionSpec as P

ITERS = 6
LOWER = 1.0
UPPER = 14.0
CENTRE = (UPPER + LOWER) / 2.0
RADIUS = (UPPER - LOWER) / 2.0
BF16 = jnp.bfloat16
F32 = jnp.float32
PARTS = 2
VMEM_BYTES = 24 * 1024 * 1024


def chebyshev_factors():
    spread = CENTRE / RADIUS
    rho = 1.0 / spread
    factors = []
    for _ in range(ITERS - 1):
        rho_new = 1.0 / (2.0 * spread - rho)
        factors.append((rho_new * rho, 2.0 * rho_new / RADIUS))
        rho = rho_new
    return factors


def pairings(groups, owners):
    found = []
    for first in (0, 1):
        route = []
        for g in range(groups):
            for s in range(owners):
                t = s + 1 if (s - first) % 2 == 0 else s - 1
                h = g
                if t < 0 or t >= owners:
                    t = s
                    h = g ^ 1
                if h < groups:
                    route.append((g * owners + s, h * owners + t))
        found.append(route)
    return found


def halves(x):
    high = x.astype(BF16)
    return high, (x - high.astype(F32)).astype(BF16)


def operand(x):
    high, low = halves(x)
    return jnp.concatenate([high, low], axis=0), high


def split_dot(cases, matrix):
    both, high = cases
    h = matrix.shape[0] // 2
    tall = jnp.dot(both, matrix[:h], preferred_element_type=F32)
    rows = high.shape[0]
    return tall[:rows] + tall[rows:] + jnp.dot(high, matrix[h:], preferred_element_type=F32)


def dot_nt(a, b):
    return lax.dot_general(a, b, (((1,), (1,)), ((), ())), preferred_element_type=F32)


def signed_placement(pairs):
    h = pairs.shape[1]
    rows = lax.broadcasted_iota(jnp.int32, (h, h), 0)
    picked = jnp.abs(pairs) - 1
    sign = jnp.where(pairs > 0, 1.0, -1.0)
    return jnp.where(rows == picked, sign, 0.0).astype(BF16)


def exists_of(count, pos, owners, slot):
    there = jnp.logical_and(slot < count, jnp.logical_or(pos < owners - 1, slot != count - 1))
    return jnp.where(there, 1.0, 0.0)


def row(marks, k):
    return marks[k, pl.ds(0, 1), :]


def first_kernel(owners, operators, counts, pairs, gap, upper_left, lower_left, residual, direction, ahead_out, even_out, odd_out, marks, pairs_at, top, source, sems):
    slots, h = residual.shape[0], residual.shape[2]
    copies = [
        pltpu.make_async_copy(pairs.at[0, 0], pairs_at, sems.at[0]),
        pltpu.make_async_copy(operators.at[0, 0, 0, pl.ds(0, h)], top, sems.at[1]),
        pltpu.make_async_copy(gap.at[0, 0], source, sems.at[2]),
    ]
    for copy in copies:
        copy.start()
    pos = lax.axis_index("sub")
    count = counts[0, 0]
    is_even = lax.rem(pos, 2) == 0
    shape = marks.shape[1:]
    for j in range(slots):
        here = exists_of(count, pos, owners, j)
        marks[j] = jnp.full(shape, jnp.where(count - 1 == j, here, 0.0), F32)
        marks[slots + 1 + j] = jnp.full(shape, jnp.where(pos == 0, 0.0, here) if j == 0 else here, F32)
    marks[slots] = jnp.full(shape, jnp.where(is_even, 1.0, 0.0), F32)
    copies[0].wait()
    place = signed_placement(pairs_at[pl.ds(0, 1), :])
    copies[1].wait()
    placed = [jnp.dot(place, part, preferred_element_type=F32).astype(BF16) for part in halves(top[...])]
    square = [dot_nt(place, part[:, :h]) for part in placed]
    square = square[0] + square[1]
    upper_left[...] = square[: h // 2]
    lower_left[...] = square[h // 2 :]
    copies[2].wait()
    for j in range(slots):
        residual[j] = source[j].T * exists_of(count, pos, owners, j)
        direction[j] = residual[j] / CENTRE
    both, high = operand(direction[0])
    tall = dot_nt(both, placed[0][:, h:])
    rows = high.shape[0]
    behind = -(tall[:rows] + tall[rows:] + dot_nt(high, placed[1][:, h:]))
    ahead = direction[count - 1]
    ahead_out[...] = ahead
    even_out[...] = jnp.where(is_even, ahead, behind)
    odd_out[...] = jnp.where(is_even, behind, ahead)


def operator_kernel(operators, pairs, marks, own_out, lower_out, upper_out, whole, sems):
    slots, h = pairs.shape
    copies = [pltpu.make_async_copy(operators.at[0, 0, j], whole.at[j], sems.at[j]) for j in range(slots)]
    for copy in copies:
        copy.start()
    unit = signed_placement(lax.broadcasted_iota(jnp.int32, (1, h), 1) + 1)
    for j in range(slots):
        copies[j].wait()
        place = signed_placement(pairs[pl.ds(j, 1), :])
        taken = marks[slots + 1 + j, pl.ds(0, 1), pl.ds(0, 1)]
        squares, diagonal = [], []
        for k, part in enumerate(halves(whole[j])):
            rows = pl.ds(k * h, h)
            placed = jnp.dot(place, part[:h], preferred_element_type=F32).astype(BF16)
            upper_out[j, rows, :] = -dot_nt(unit, placed[:, h:]).astype(BF16)
            lower_out[j, rows, :] = (dot_nt(place, part[h:, :h]) * -taken).astype(BF16)
            squares.append(dot_nt(place, placed[:, :h]))
            diagonal.append(dot_nt(unit, part[h:, h:]))
        if j > 0:
            before = marks[j - 1, pl.ds(0, 1), pl.ds(0, 1)]
            put_halves(own_out, j - 1, previous + jnp.where(before > 0.5, 0.0, squares[0] + squares[1]))
        previous = diagonal[0] + diagonal[1]
    put_halves(own_out, slots - 1, previous)


def put_halves(out, j, matrix):
    h = matrix.shape[0]
    out[j, pl.ds(0, h), :], out[j, pl.ds(h, h), :] = halves(matrix)


def inner_step(own, lower, upper, marks, direction, residual, factors, residual_out, first_part, last_part):
    slots = len(direction)
    cases = [operand(block) for block in direction]
    last, last_residual = 0.0, 0.0
    for j in range(slots):
        image = split_dot(cases[j], own[j])
        if j > 0:
            image += split_dot(cases[j - 1], lower[j])
        if j + 1 < slots:
            image += split_dot(cases[j + 1], upper[j + 1])
        rest = residual[j] - image
        if factors is None:
            residual_out[j] = rest.T
            continue
        residual_out[j] = rest
        if j == 0:
            first_part[...] = factors[0] * direction[0] + factors[1] * rest
        last += row(marks, j) * direction[j]
        last_residual += row(marks, j) * rest
    if factors is not None:
        last_part[...] = factors[0] * last + factors[1] * last_residual


def first_inner_kernel(factors, own, lower, upper, marks, direction, residual, residual_out, first_part, last_part):
    slots = direction.shape[0]
    blocks, rests = [direction[j] for j in range(slots)], [residual[j] for j in range(slots)]
    inner_step(own, lower, upper, marks, blocks, rests, factors, residual_out, first_part, last_part)


def inner_kernel(before, factors, joins, parts, own, lower, upper, marks, direction, residual, total, *rest):
    rest = list(rest)
    slots, h = direction.shape[0], direction.shape[2]
    across = jnp.concatenate([part[...] for part in rest[:parts]], axis=0)
    behind = jnp.concatenate([part[...] for part in rest[parts : 2 * parts]], axis=0)
    rest = rest[2 * parts :]
    if joins:
        left = jnp.concatenate([rest[0][...], rest[1][...]], axis=0)
        joined = rest[-1]
        rest = rest[2:-1]
        for j in range(slots):
            matrix = own[j, pl.ds(0, h), :].astype(F32) + own[j, pl.ds(h, h), :].astype(F32)
            put_halves(joined, j, matrix + left * marks[j, pl.ds(0, 1), pl.ds(0, 1)])
        own = joined
    residual_out, total_out = rest[:2]
    direction_out, first_part, last_part = rest[2:] if factors is not None else (None, None, None)
    blocks, rests = [], []
    for j in range(slots):
        left_over = residual[j] - row(marks, j) * behind
        if j == 0:
            left_over -= across
        block = before[0] * direction[j] + before[1] * left_over
        if direction_out is not None:
            direction_out[j] = block
            total_out[j] = total[j] + block
        else:
            total_out[j] = (total[j] + block).T
        blocks.append(block)
        rests.append(left_over)
    inner_step(own, lower, upper, marks, blocks, rests, factors, residual_out, first_part, last_part)


def received(marks, even, odd, slots):
    is_even = row(marks, slots) > 0.5
    return jnp.where(is_even, odd, even), jnp.where(is_even, even, odd)


def edge_kernel(factors, joins, start, outs, lower, upper, marks, even_in, odd_in, first_part, last_part, *rest):
    slots = lower.shape[0]
    if joins:
        upper_left, lower_left, ahead, *rest = rest
    across_out, behind_out, *sent_out = rest
    rows = pl.ds(start, even_in.shape[0])
    before, behind = received(marks, even_in[...], odd_in[...], slots)
    across = split_dot(operand(before), lower[0])
    if joins:
        left = jnp.concatenate([upper_left[...], lower_left[...]], axis=0)
        behind += split_dot(operand(ahead[...]), jnp.concatenate(halves(left), axis=0))
    across_out[...] = across
    behind_out[...] = behind
    exists = sum(row(marks, j) for j in range(slots))
    alone = row(marks, 0)
    first = first_part[rows, :] - factors[1] * (across + alone * behind)
    last = last_part[rows, :] - factors[1] * (exists * behind + alone * across)
    sent = split_dot(operand(first), upper[0])
    is_even = row(marks, slots) > 0.5
    even, odd = jnp.where(is_even, last, sent), jnp.where(is_even, sent, last)
    height = even.shape[0] // outs
    for k in range(outs):
        sent_out[2 * k][...] = even[k * height : (k + 1) * height]
        sent_out[2 * k + 1][...] = odd[k * height : (k + 1) * height]


def last_kernel(parts, lower, marks, *rest):
    slots = lower.shape[0]
    even = jnp.concatenate([part[...] for part in rest[:parts]], axis=0)
    odd = jnp.concatenate([part[...] for part in rest[parts : 2 * parts]], axis=0)
    residual, out, ready, sems = rest[2 * parts :]
    before, behind = received(marks, even, odd, slots)
    behind = behind.T
    copies = [pltpu.make_async_copy(ready.at[j], out.at[0, 0, j], sems.at[j]) for j in range(slots)]
    for j in range(1, slots):
        ready[j] = residual[j] - marks[j, pl.ds(0, 1), pl.ds(0, behind.shape[1])] * behind
        copies[j].start()
    across = split_dot(operand(before), lower[0])
    ready[0] = residual[0] - marks[0, pl.ds(0, 1), pl.ds(0, behind.shape[1])] * behind - across.T
    copies[0].start()
    for copy in copies:
        copy.wait()


VMEM = pl.BlockSpec(memory_space=pltpu.VMEM)
SMEM = pl.BlockSpec(memory_space=pltpu.SMEM)
HBM = pl.BlockSpec(memory_space=pltpu.HBM)


def in_hbm(x):
    return pltpu.with_memory_space_constraint(x, pltpu.HBM)


def call(kernel, name, ins, outs, scratch=(), out_space=VMEM):
    return pl.pallas_call(
        kernel,
        in_specs=ins,
        out_specs=[out_space] * len(outs),
        out_shape=[jax.ShapeDtypeStruct(shape, kind) for shape, kind in outs],
        scratch_shapes=list(scratch),
        compiler_params=pltpu.CompilerParams(vmem_limit_bytes=VMEM_BYTES),
        name=name,
    )


def shards(groups, owners, operators, counts, pair_rows, gap):
    slots, h, cases = gap.shape[2:]
    m = operators.shape[-1]
    width = cases // PARTS
    evens, odds = pairings(groups, owners)
    ring = [((s + 1) % owners, s) for s in range(owners)]
    field = ((slots, cases, h), F32)
    turned = ((slots, h, cases), F32)
    block = ((cases, h), F32)
    part = ((width, h), F32)
    matrices = ((slots, 2 * h, h), BF16)

    def exchange(even, odd):
        odd = lax.ppermute(odd, ("grp", "sub"), odds)
        even = lax.ppermute(even, ("grp", "sub"), evens)
        return even, odd

    operators = in_hbm(operators)
    *lefts, residual, direction, ahead, even, odd, marks = call(
        functools.partial(first_kernel, owners),
        "first_messages",
        [HBM, SMEM, HBM, HBM],
        [((h // 2, h), F32)] * 2 + [field, field, block, block, block, ((2 * slots + 1, 8, h), F32)],
        [
            pltpu.VMEM((slots, h), jnp.int32),
            pltpu.VMEM((h, m), F32),
            pltpu.VMEM(*turned),
            pltpu.SemaphoreType.DMA((3,)),
        ],
    )(operators, counts, in_hbm(pair_rows), in_hbm(gap))
    sent = [exchange(even, odd)]
    lefts = [lax.ppermute(half, "sub", ring) for half in lefts]
    own, lower, upper = call(
        operator_kernel,
        "block_operators",
        [HBM, VMEM, VMEM],
        [matrices] * 3,
        [pltpu.VMEM((slots, m, m), F32), pltpu.SemaphoreType.DMA((slots,))],
    )(operators, pair_rows[0, 0], marks)
    factors = chebyshev_factors() + [None]
    residual, first, last = call(
        functools.partial(first_inner_kernel, factors[0]), "first_inner_blocks", [VMEM] * 6, [field, block, block]
    )(own, lower, upper, marks, direction, residual)
    total = direction
    for step in range(1, ITERS):
        joins = step == 1
        extra = [*lefts, ahead] if joins else []
        across, behind, sending = [], [], []
        for k, (even, odd) in enumerate(sent):
            outs = PARTS if joins else 1
            got = call(
                functools.partial(edge_kernel, factors[step - 1], joins, k * width, outs),
                "edge_blocks",
                [VMEM] * (7 + len(extra)),
                [block if joins else part] * 2 + [part] * (2 * outs),
            )(lower, upper, marks, even, odd, first, last, *extra)
            across.append(got[0])
            behind.append(got[1])
            sending += [exchange(got[2 + 2 * n], got[3 + 2 * n]) for n in range(outs)]
        sent = sending
        extra = lefts if joins else []
        ends = step == ITERS - 1
        outs = ([turned] * 2 if ends else [field] * 3 + [block] * 2) + ([matrices] if joins else [])
        got = call(
            functools.partial(inner_kernel, factors[step - 1], factors[step], joins, len(across)),
            "inner_blocks",
            [VMEM] * (7 + 2 * len(across) + len(extra)),
            outs,
        )(own, lower, upper, marks, direction, residual, total, *across, *behind, *extra)
        residual, total = got[:2]
        if not ends:
            direction, first, last = got[2:5]
        if joins:
            own = got[5]
    (residual,) = call(
        functools.partial(last_kernel, PARTS),
        "last_residual",
        [VMEM] * (3 + 2 * PARTS),
        [(gap.shape, F32)],
        [pltpu.VMEM(*turned), pltpu.SemaphoreType.DMA((slots,))],
        HBM,
    )(lower, marks, *(even for even, _ in sent), *(odd for _, odd in sent), residual)
    return total[None, None], residual


def solution(mesh):
    groups, owners = mesh.shape["grp"], mesh.shape["sub"]
    return jax.shard_map(
        functools.partial(shards, groups, owners),
        mesh=mesh,
        in_specs=(
            P("grp", "sub", None, None, None),
            P("grp", "sub"),
            P("grp", "sub", None, None),
            P("grp", "sub", None, None, None),
        ),
        out_specs=(P("grp", "sub", None, None, None), P("grp", "sub", None, None, None)),
        check_vma=False,
    )
```

```python
import functools

import jax
import jax.numpy as jnp
from jax import lax
from jax.experimental import pallas as pl
from jax.experimental.pallas import tpu as pltpu
from jax.sharding import PartitionSpec as P

ITERS = 6
LOWER = 1.0
UPPER = 14.0
CENTRE = (UPPER + LOWER) / 2.0
RADIUS = (UPPER - LOWER) / 2.0
BF16 = jnp.bfloat16
F32 = jnp.float32
PARTS = 2
VMEM_BYTES = 24 * 1024 * 1024
FIRST_VMEM_BYTES = 51 * 1024 * 1024


def chebyshev_factors():
    spread = CENTRE / RADIUS
    rho = 1.0 / spread
    factors = []
    for _ in range(ITERS - 1):
        rho_new = 1.0 / (2.0 * spread - rho)
        factors.append((rho_new * rho, 2.0 * rho_new / RADIUS))
        rho = rho_new
    return factors


def pairings(groups, owners):
    found = []
    for first in (0, 1):
        route = []
        for g in range(groups):
            for s in range(owners):
                t = s + 1 if (s - first) % 2 == 0 else s - 1
                h = g
                if t < 0 or t >= owners:
                    t = s
                    h = g ^ 1
                if h < groups:
                    route.append((g * owners + s, h * owners + t))
        found.append(route)
    return found


def halves(x):
    high = x.astype(BF16)
    return high, (x - high.astype(F32)).astype(BF16)


def operand(x):
    high, low = halves(x)
    return jnp.concatenate([high, low], axis=0), high


def split_dot(cases, matrix):
    both, high = cases
    h = matrix.shape[0] // 2
    tall = jnp.dot(both, matrix[:h], preferred_element_type=F32)
    rows = high.shape[0]
    return tall[:rows] + tall[rows:] + jnp.dot(high, matrix[h:], preferred_element_type=F32)


def dot_nt(a, b):
    return lax.dot_general(a, b, (((1,), (1,)), ((), ())), preferred_element_type=F32)


def signed_placement(pairs):
    h = pairs.shape[1]
    rows = lax.broadcasted_iota(jnp.int32, (h, h), 0)
    picked = jnp.abs(pairs) - 1
    sign = jnp.where(pairs > 0, 1.0, -1.0)
    return jnp.where(rows == picked, sign, 0.0).astype(BF16)


def row(marks, k):
    return marks[k, pl.ds(0, 1), :]


def mark_places(slots):
    return dict(even=slots, alone=slots + 1, evens=slots + 2, odds=slots + 3)


def first_kernel(owners, counts, operators, pairs, gap, residual, direction, ends, beside_even, beside_odd, marks, pairs_out, source, sems):
    slots = source.shape[0]
    copies = [
        pltpu.make_async_copy(gap.at[0, 0], source, sems.at[0]),
        pltpu.make_async_copy(pairs.at[0, 0], pairs_out, sems.at[1]),
    ]
    for copy in copies:
        copy.start()
    pos = lax.axis_index("sub")
    count = counts[0, 0]
    is_even = lax.rem(pos, 2) == 0
    place = mark_places(slots)
    has_left, has_right = pos > 0, pos < owners - 1
    flags = [count - 1 == j for j in range(slots)] + [None] * 4
    flags[place["even"]] = is_even
    flags[place["alone"]] = count == 1
    flags[place["evens"]] = jnp.logical_or(jnp.logical_and(is_even, has_right), jnp.logical_and(~is_even, has_left))
    flags[place["odds"]] = jnp.logical_or(jnp.logical_and(is_even, has_left), jnp.logical_and(~is_even, has_right))
    for k, flag in enumerate(flags):
        marks[k] = jnp.full(marks.shape[1:], jnp.where(flag, 1.0, 0.0), F32)
    copies[0].wait()
    ends[...] = source[count - 1].T * jnp.where(has_right, 1.0, 0.0)
    for j in range(slots - 1):
        residual[j] = source[j].T * jnp.where(j < count - 1, 1.0, 0.0)
        direction[j] = residual[j] / CENTRE
    put_beside(marks, slots, [direction[j] for j in range(slots - 1)], beside_even, beside_odd)
    copies[1].wait()


def put_beside(marks, slots, blocks, beside_even, beside_odd):
    is_even = row(marks, mark_places(slots)["even"]) > 0.5
    first, before_last = blocks[0], sum(row(marks, j + 1) * blocks[j] for j in range(slots - 1))
    beside_even[...] = jnp.where(is_even, before_last, first)
    beside_odd[...] = jnp.where(is_even, first, before_last)


def operator_kernel(counts, operators, pairs, own_out, lower_out, upper_out, even_out, odd_out):
    slots, h = pairs.shape
    count = counts[0, 0]
    is_even = lax.rem(lax.axis_index("sub"), 2) == 0
    unit = signed_placement(lax.broadcasted_iota(jnp.int32, (1, h), 1) + 1)
    for j in range(slots):
        place = signed_placement(pairs[pl.ds(j, 1), :])
        between = jnp.where(j < count - 1, 1.0, 0.0)
        squares, diagonal, lowers, uppers = [], [], [], []
        for part in halves(operators[0, 0, j]):
            placed = jnp.dot(place, part[:h], preferred_element_type=F32).astype(BF16)
            uppers.append(-dot_nt(unit, placed[:, h:]).astype(BF16))
            lowers.append(-dot_nt(place, part[h:, :h]))
            squares.append(dot_nt(place, placed[:, :h]))
            diagonal.append(dot_nt(unit, part[h:, h:]))
        for k in range(2):
            rows = pl.ds(k * h, h)
            if j < slots - 1:
                lower_out[j, rows, :] = (lowers[k] * between).astype(BF16)
            if j > 0:
                upper_out[j - 1, rows, :] = uppers[k]

            def put_end(out, square, other, rows=rows, k=k):
                out[0, rows, :] = square[k].astype(BF16)
                out[1, rows, :] = other[k].astype(BF16)

            if j == 0:
                pl.when(is_even)(functools.partial(put_end, odd_out, squares, uppers))
                pl.when(~is_even)(functools.partial(put_end, even_out, squares, uppers))
            is_last = count - 1 == j
            pl.when(jnp.logical_and(is_last, is_even))(functools.partial(put_end, even_out, diagonal, lowers))
            pl.when(jnp.logical_and(is_last, ~is_even))(functools.partial(put_end, odd_out, diagonal, lowers))
        if j > 0:
            summed = (previous + (squares[0] + squares[1])) * jnp.where(j < count, 1.0, 0.0)
            own_out[j - 1, pl.ds(0, h), :], own_out[j - 1, pl.ds(h, h), :] = halves(summed)
        previous = diagonal[0] + diagonal[1]


def give(marks, slots, even, odd, beside_even, beside_odd, even_operator, odd_operator):
    alone = row(marks, mark_places(slots)["alone"]) > 0.5
    next_even, next_odd = jnp.where(alone, odd, beside_even), jnp.where(alone, even, beside_odd)
    return (
        split_dot(operand(even), even_operator[0]) + split_dot(operand(next_even), even_operator[1]),
        split_dot(operand(odd), odd_operator[0]) + split_dot(operand(next_odd), odd_operator[1]),
    )


def first_edge_kernel(slots, parts, even_operator, odd_operator, marks, ends, before, beside_even, beside_odd, *outs):
    place = mark_places(slots)
    is_even = row(marks, place["even"]) > 0.5
    even = jnp.where(is_even, ends[...], before[...]) * row(marks, place["evens"])
    odd = jnp.where(is_even, before[...], ends[...]) * row(marks, place["odds"])
    directions = even / CENTRE, odd / CENTRE
    given = give(marks, slots, *directions, beside_even[...], beside_odd[...], even_operator, odd_operator)
    height = even.shape[0] // parts
    for k in range(parts):
        for n, x in enumerate((even, odd, *directions, *given)):
            outs[6 * k + n][...] = x[k * height : (k + 1) * height]


def edge_kernel(factors, slots, start, ends, even_operator, odd_operator, marks, beside_even, beside_odd, *refs):
    even_r, odd_r, even_v, odd_v, even_sent, odd_sent, even_in, odd_in = (ref[...] for ref in refs[:8])
    outs = refs[8:]
    place = mark_places(slots)
    rows = pl.ds(start, even_r.shape[0])
    even_r = (even_r - (even_sent + even_in)) * row(marks, place["evens"])
    odd_r = (odd_r - (odd_sent + odd_in)) * row(marks, place["odds"])
    even_v = factors[0] * even_v + factors[1] * even_r
    odd_v = factors[0] * odd_v + factors[1] * odd_r
    given = give(marks, slots, even_v, odd_v, beside_even[rows, :], beside_odd[rows, :], even_operator, odd_operator)
    if ends:
        is_even = row(marks, place["even"]) > 0.5
        last_r, last_given = jnp.where(is_even, even_r, odd_r), jnp.where(is_even, given[0], given[1])
        results = last_r, last_given, even_v, odd_v, jnp.where(is_even, given[1], given[0])
    else:
        results = even_r, odd_r, even_v, odd_v, *given
    for out, x in zip(outs, results):
        out[...] = x


def inner_kernel(factors, parts, own, lower, upper, marks, direction, residual, *rest):
    rest = list(rest)
    inner = residual.shape[0]
    slots = inner + 1
    even = jnp.concatenate([ref[...] for ref in rest[:parts]], axis=0)
    odd = jnp.concatenate([ref[...] for ref in rest[parts : 2 * parts]], axis=0)
    total, *outs = rest[2 * parts :]
    is_even = row(marks, mark_places(slots)["even"]) > 0.5
    last, before = jnp.where(is_even, even, odd), jnp.where(is_even, odd, even)
    blocks = [row(marks, j) * last + (direction[j] if j < inner else 0.0) for j in range(slots)]
    cases = [operand(block) for block in blocks]
    residual_out, total_out = outs[:2]
    for j in range(slots):
        summed = total[j] + blocks[j]
        total_out[j] = summed if factors is not None else summed.T
    nexts = []
    for j in range(inner):
        image = split_dot(cases[j], own[j]) + split_dot(cases[j + 1], upper[j])
        image += split_dot(cases[j - 1] if j > 0 else operand(before), lower[j])
        left_over = residual[j] - image
        if factors is None:
            residual_out[j] = left_over.T
            continue
        residual_out[j] = left_over
        nexts.append(factors[0] * direction[j] + factors[1] * left_over)
        outs[2][j] = nexts[j]
    if factors is not None:
        put_beside(marks, slots, nexts, outs[3], outs[4])


def last_kernel(parts, marks, residual, *refs):
    out, ready, sems = refs[3 * parts :]
    inner = residual.shape[0]
    slots = inner + 1
    place = mark_places(slots)
    last_r, last_given, came = (
        jnp.concatenate([ref[...] for ref in refs[n * parts : (n + 1) * parts]], axis=0) for n in range(3)
    )
    is_even = row(marks, place["even"]) > 0.5
    shared = jnp.where(is_even, row(marks, place["evens"]), row(marks, place["odds"]))
    last = ((last_r - (last_given + came)) * shared).T
    copies = []
    for j in range(slots):
        mine = marks[j, pl.ds(0, 1), pl.ds(0, last.shape[1])] * last
        ready[j] = mine + residual[j] if j < inner else mine
        copies.append(pltpu.make_async_copy(ready.at[j], out.at[0, 0, j], sems.at[j]))
        copies[j].start()
    for copy in copies:
        copy.wait()


VMEM = pl.BlockSpec(memory_space=pltpu.VMEM)
SMEM = pl.BlockSpec(memory_space=pltpu.SMEM)
HBM = pl.BlockSpec(memory_space=pltpu.HBM)


def in_hbm(x):
    return pltpu.with_memory_space_constraint(x, pltpu.HBM)


def call(kernel, name, ins, outs, scratch=(), out_space=VMEM, vmem=VMEM_BYTES):
    return pl.pallas_call(
        kernel,
        in_specs=ins,
        out_specs=[out_space] * len(outs),
        out_shape=[jax.ShapeDtypeStruct(shape, kind) for shape, kind in outs],
        scratch_shapes=list(scratch),
        compiler_params=pltpu.CompilerParams(vmem_limit_bytes=vmem),
        name=name,
    )


def shards(groups, owners, operators, counts, pair_rows, gap):
    slots, h, cases = gap.shape[2:]
    width = cases // PARTS
    evens, odds = pairings(groups, owners)
    forward = [(s, (s + 1) % owners) for s in range(owners)]
    backward = [(t, s) for s, t in forward]
    field = ((slots, cases, h), F32)
    inner = ((slots - 1, cases, h), F32)
    block = ((cases, h), F32)
    part = ((width, h), F32)
    matrices = ((slots - 1, 2 * h, h), BF16)
    pair = ((2, 2 * h, h), BF16)

    def exchange(even, odd):
        odd = lax.ppermute(odd, ("grp", "sub"), odds)
        even = lax.ppermute(even, ("grp", "sub"), evens)
        return even, odd

    residual, direction, ends, *beside, marks, pairs = call(
        functools.partial(first_kernel, owners),
        "first_blocks",
        [SMEM, HBM, HBM, HBM],
        [inner, inner, block, block, block, ((slots + 4, 8, h), F32), ((slots, h), jnp.int32)],
        [pltpu.VMEM((slots, h, cases), F32), pltpu.SemaphoreType.DMA((2,))],
        vmem=FIRST_VMEM_BYTES,
    )(counts, operators, in_hbm(pair_rows), in_hbm(gap))
    before = lax.ppermute(ends, "sub", forward)
    own, lower, upper, even_operator, odd_operator = call(
        operator_kernel,
        "block_operators",
        [SMEM, VMEM, VMEM],
        [matrices] * 3 + [pair] * 2,
    )(counts, operators, pairs)
    got = call(
        functools.partial(first_edge_kernel, slots, PARTS), "first_edges", [VMEM] * 7, [part] * (6 * PARTS)
    )(even_operator, odd_operator, marks, ends, before, *beside)
    states = [got[6 * k : 6 * k + 6] for k in range(PARTS)]
    total = jnp.zeros(field[0], F32)
    for step, factors in enumerate(chebyshev_factors() + [None]):
        if factors is None:
            came = [lax.ppermute(state[4], "sub", backward) for state in states]
        else:
            came = [exchange(state[4], state[5]) for state in states]
        outs = [inner, field, inner, block, block]
        if factors is None:
            outs = [((slots - 1, h, cases), F32), ((slots, h, cases), F32)]
        got = call(
            functools.partial(inner_kernel, factors, PARTS), "inner_blocks", [VMEM] * (7 + 2 * PARTS), outs
        )(own, lower, upper, marks, direction, residual, *(s[2] for s in states), *(s[3] for s in states), total)
        residual, total = got[:2]
        if factors is not None:
            direction, *beside = got[2:]
            states = [
                call(
                    functools.partial(edge_kernel, factors, slots, k * width, step == ITERS - 2),
                    "edge_blocks",
                    [VMEM] * 13,
                    [part] * (5 if step == ITERS - 2 else 6),
                )(even_operator, odd_operator, marks, *beside, *states[k], *came[k])
                for k in range(PARTS)
            ]
    (residual,) = call(
        functools.partial(last_kernel, PARTS),
        "last_residual",
        [VMEM] * (2 + 3 * PARTS),
        [(gap.shape, F32)],
        [pltpu.VMEM((slots, h, cases), F32), pltpu.SemaphoreType.DMA((slots,))],
        HBM,
    )(marks, residual, *(s[n] for n in (0, 1) for s in states), *came)
    return total[None, None], residual


def solution(mesh):
    groups, owners = mesh.shape["grp"], mesh.shape["sub"]
    return jax.shard_map(
        functools.partial(shards, groups, owners),
        mesh=mesh,
        in_specs=(
            P("grp", "sub", None, None, None),
            P("grp", "sub"),
            P("grp", "sub", None, None),
            P("grp", "sub", None, None, None),
        ),
        out_specs=(P("grp", "sub", None, None, None), P("grp", "sub", None, None, None)),
        check_vma=False,
    )
```

```python
import functools

import jax
import jax.numpy as jnp
from jax import lax
from jax.experimental import pallas as pl
from jax.experimental.pallas import tpu as pltpu
from jax.sharding import PartitionSpec as P

ITERS = 6
LOWER = 1.0
UPPER = 14.0
CENTRE = (UPPER + LOWER) / 2.0
RADIUS = (UPPER - LOWER) / 2.0
BF16 = jnp.bfloat16
F32 = jnp.float32
PARTS = 2
VMEM_BYTES = 24 * 1024 * 1024
FIRST_VMEM_BYTES = 52 * 1024 * 1024


def chebyshev_factors():
    spread = CENTRE / RADIUS
    rho = 1.0 / spread
    factors = []
    for _ in range(ITERS - 1):
        rho_new = 1.0 / (2.0 * spread - rho)
        factors.append((rho_new * rho, 2.0 * rho_new / RADIUS))
        rho = rho_new
    return factors


def pairings(groups, owners):
    found = []
    for first in (0, 1):
        route = []
        for g in range(groups):
            for s in range(owners):
                t = s + 1 if (s - first) % 2 == 0 else s - 1
                h = g
                if t < 0 or t >= owners:
                    t = s
                    h = g ^ 1
                if h < groups:
                    route.append((g * owners + s, h * owners + t))
        found.append(route)
    return found


def halves(x):
    high = x.astype(BF16)
    return high, (x - high.astype(F32)).astype(BF16)


def operand(x):
    high, low = halves(x)
    return jnp.concatenate([high, low], axis=0), high


def split_dot(cases, matrix):
    both, high = cases
    h = matrix.shape[0] // 2
    tall = jnp.dot(both, matrix[:h], preferred_element_type=F32)
    rows = high.shape[0]
    return tall[:rows] + tall[rows:] + jnp.dot(high, matrix[h:], preferred_element_type=F32)


def beside(x, y):
    return tuple(jnp.concatenate(pair, axis=1) for pair in zip(x, y))


def dot_nt(a, b):
    return lax.dot_general(a, b, (((1,), (1,)), ((), ())), preferred_element_type=F32)


def signed_placement(pairs, scale):
    h = pairs.shape[1]
    rows = lax.broadcasted_iota(jnp.int32, (h, h), 0)
    return jnp.where(rows == jnp.abs(pairs) - 1, jnp.where(pairs > 0, scale, -scale), 0.0).astype(BF16)


def row(marks, k):
    return marks[k, pl.ds(0, 1), :]


def mark_places(slots):
    return dict(even=slots, alone=slots + 1, evens=slots + 2, odds=slots + 3)


def first_kernel(owners, counts, operators, pairs, gap, ends, marks, pairs_out, source, sems):
    slots = pairs_out.shape[0]
    count = counts[0, 0]
    copies = [
        pltpu.make_async_copy(gap.at[0, 0, count - 1], source, sems.at[0]),
        pltpu.make_async_copy(pairs.at[0, 0], pairs_out, sems.at[1]),
    ]
    for copy in copies:
        copy.start()
    pos = lax.axis_index("sub")
    is_even = lax.rem(pos, 2) == 0
    place = mark_places(slots)
    has_left, has_right = pos > 0, pos < owners - 1
    flags = [count - 1 == j for j in range(slots)] + [None] * 4
    flags[place["even"]] = is_even
    flags[place["alone"]] = count == 1
    flags[place["evens"]] = jnp.logical_or(jnp.logical_and(is_even, has_right), jnp.logical_and(~is_even, has_left))
    flags[place["odds"]] = jnp.logical_or(jnp.logical_and(is_even, has_left), jnp.logical_and(~is_even, has_right))
    for k, flag in enumerate(flags):
        marks[k] = jnp.full(marks.shape[1:], jnp.where(flag, 1.0, 0.0), F32)
    copies[0].wait()
    ends[...] = source[...].T * jnp.where(has_right, 1.0, 0.0)
    copies[1].wait()


def put_beside(marks, slots, blocks, beside_even, beside_odd):
    is_even = row(marks, mark_places(slots)["even"]) > 0.5
    first, before_last = blocks[0], sum(row(marks, j + 1) * blocks[j] for j in range(slots - 1))
    beside_even[...] = jnp.where(is_even, before_last, first)
    beside_odd[...] = jnp.where(is_even, first, before_last)


def operator_kernel(counts, operators, pairs, marks, gap, own_out, lower_out, upper_out, even_out, odd_out, residual, direction, beside_even, beside_odd, source, sem):
    slots, h = pairs.shape
    count = counts[0, 0]
    copy = pltpu.make_async_copy(gap.at[0, 0, pl.ds(0, slots - 1)], source, sem)
    copy.start()
    is_even = lax.rem(lax.axis_index("sub"), 2) == 0
    low = pl.ds(h, h)
    for j in range(slots):
        row_pairs = pairs[pl.ds(j, 1), :]
        place = signed_placement(row_pairs, 1.0)
        parts = halves(operators[0, 0, j])
        placed = [jnp.dot(place, part[:h], preferred_element_type=F32) for part in parts]
        uppers = [(-part[:, h:]).T.astype(BF16) for part in placed]
        placed = [part[:, :h].astype(BF16) for part in placed]
        if j > 0:
            live = jnp.where(j < count, 1.0, 0.0)
            scaled = signed_placement(row_pairs, live)
            square = dot_nt(jnp.concatenate([scaled, scaled], axis=1), jnp.concatenate(placed, axis=1))
            put_halves(own_out, j - 1, square + operators[0, 0, j - 1, low, low].T * live)
            upper_out[j - 1, pl.ds(0, h), :], upper_out[j - 1, low, :] = uppers
        if j < slots - 1:
            scaled = signed_placement(row_pairs, jnp.where(j < count - 1, -1.0, 0.0))
            for k, part in enumerate(parts):
                lower_out[j, pl.ds(k * h, h), :] = dot_nt(scaled, part[h:, :h]).astype(BF16)

        def put_first(out, place=place, placed=placed, uppers=uppers):
            for k in range(2):
                out[pl.ds(2 * k * h, h), :] = dot_nt(place, placed[k]).astype(BF16)
                out[pl.ds((2 * k + 1) * h, h), :] = uppers[k]

        def put_last(out, j=j, row_pairs=row_pairs, parts=parts):
            out[pl.ds(0, h), :], out[pl.ds(2 * h, h), :] = halves(operators[0, 0, j, low, low].T)
            turned = signed_placement(row_pairs, -1.0)
            for k, part in enumerate(parts):
                out[pl.ds((2 * k + 1) * h, h), :] = dot_nt(turned, part[h:, :h]).astype(BF16)

        if j == 0:
            pl.when(is_even)(functools.partial(put_first, odd_out))
            pl.when(~is_even)(functools.partial(put_first, even_out))
        is_last = count - 1 == j
        pl.when(jnp.logical_and(is_last, is_even))(functools.partial(put_last, even_out))
        pl.when(jnp.logical_and(is_last, ~is_even))(functools.partial(put_last, odd_out))
    copy.wait()
    for j in range(slots - 1):
        residual[j] = source[j].T * jnp.where(j < count - 1, 1.0, 0.0)
        direction[j] = residual[j] / CENTRE
    put_beside(marks, slots, [direction[j] for j in range(slots - 1)], beside_even, beside_odd)


def put_halves(out, j, matrix):
    h = matrix.shape[0]
    out[j, pl.ds(0, h), :], out[j, pl.ds(h, h), :] = halves(matrix)


def give(marks, slots, even, odd, beside_even, beside_odd, even_operator, odd_operator):
    alone = row(marks, mark_places(slots)["alone"]) > 0.5
    next_even, next_odd = jnp.where(alone, odd, beside_even), jnp.where(alone, even, beside_odd)
    return (
        split_dot(beside(operand(even), operand(next_even)), even_operator[...]),
        split_dot(beside(operand(odd), operand(next_odd)), odd_operator[...]),
    )


def first_edge_kernel(slots, parts, even_operator, odd_operator, marks, ends, before, beside_even, beside_odd, *outs):
    place = mark_places(slots)
    is_even = row(marks, place["even"]) > 0.5
    even = jnp.where(is_even, ends[...], before[...]) * row(marks, place["evens"])
    odd = jnp.where(is_even, before[...], ends[...]) * row(marks, place["odds"])
    directions = even / CENTRE, odd / CENTRE
    given = give(marks, slots, *directions, beside_even[...], beside_odd[...], even_operator, odd_operator)
    height = even.shape[0] // parts
    for k in range(parts):
        for n, x in enumerate((even, odd, *directions, *given)):
            outs[6 * k + n][...] = x[k * height : (k + 1) * height]


def edge_kernel(factors, slots, start, ends, even_operator, odd_operator, marks, beside_even, beside_odd, *refs):
    even_r, odd_r, even_v, odd_v, even_sent, odd_sent, even_in, odd_in = (ref[...] for ref in refs[:8])
    outs = refs[8:]
    place = mark_places(slots)
    rows = pl.ds(start, even_r.shape[0])
    even_r = (even_r - (even_sent + even_in)) * row(marks, place["evens"])
    odd_r = (odd_r - (odd_sent + odd_in)) * row(marks, place["odds"])
    even_v = factors[0] * even_v + factors[1] * even_r
    odd_v = factors[0] * odd_v + factors[1] * odd_r
    given = give(marks, slots, even_v, odd_v, beside_even[rows, :], beside_odd[rows, :], even_operator, odd_operator)
    if ends:
        is_even = row(marks, place["even"]) > 0.5
        last_r, last_given = jnp.where(is_even, even_r, odd_r), jnp.where(is_even, given[0], given[1])
        results = last_r, last_given, even_v, odd_v, jnp.where(is_even, given[1], given[0])
    else:
        results = even_r, odd_r, even_v, odd_v, *given
    for out, x in zip(outs, results):
        out[...] = x


def inner_kernel(factors, parts, own, lower, upper, marks, direction, residual, *rest):
    inner = residual.shape[0]
    slots = inner + 1
    even = jnp.concatenate([ref[...] for ref in rest[:parts]], axis=0)
    odd = jnp.concatenate([ref[...] for ref in rest[parts : 2 * parts]], axis=0)
    total, *outs = rest[2 * parts :]
    is_even = row(marks, mark_places(slots)["even"]) > 0.5
    last, before = jnp.where(is_even, even, odd), jnp.where(is_even, odd, even)
    blocks = [row(marks, j) * last + (direction[j] if j < inner else 0.0) for j in range(slots)]
    cases = [operand(block) for block in blocks]
    if factors is None:
        residual_out, total_out, residual_ready, total_ready, sems = outs
        pairs = ((total_ready, total_out), (residual_ready, residual_out))
        copies = [[pltpu.make_async_copy(x.at[j], y.at[0, 0, j], sems.at[n, j]) for j in range(slots)] for n, (x, y) in enumerate(pairs)]
    else:
        residual_out, total_out = outs[:2]
    for j in range(slots):
        summed = total[j] + blocks[j]
        if factors is None:
            total_ready[j] = summed.T
            copies[0][j].start()
        else:
            total_out[j] = summed
    nexts = []
    for j in range(inner):
        image = split_dot(cases[j], own[j]) + split_dot(cases[j + 1], upper[j])
        image += split_dot(cases[j - 1] if j > 0 else operand(before), lower[j])
        left_over = residual[j] - image
        if factors is None:
            residual_ready[j] = left_over.T
            copies[1][j].start()
            continue
        residual_out[j] = left_over
        nexts.append(factors[0] * direction[j] + factors[1] * left_over)
        outs[2][j] = nexts[j]
    if factors is not None:
        put_beside(marks, slots, nexts, outs[3], outs[4])
    else:
        residual_ready[inner] = jnp.zeros(residual_ready.shape[1:], F32)
        copies[1][inner].start()
        for copy in copies[0] + copies[1]:
            copy.wait()


def last_kernel(parts, slots, counts, marks, _, *refs):
    out, ready, sem = refs[3 * parts :]
    place = mark_places(slots)
    last_r, last_given, came = (
        jnp.concatenate([ref[...] for ref in refs[n * parts : (n + 1) * parts]], axis=0) for n in range(3)
    )
    is_even = row(marks, place["even"]) > 0.5
    shared = jnp.where(is_even, row(marks, place["evens"]), row(marks, place["odds"]))
    ready[...] = ((last_r - (last_given + came)) * shared).T
    copy = pltpu.make_async_copy(ready, out.at[0, 0, counts[0, 0] - 1], sem)
    copy.start()
    copy.wait()


VMEM = pl.BlockSpec(memory_space=pltpu.VMEM)
SMEM = pl.BlockSpec(memory_space=pltpu.SMEM)
HBM = pl.BlockSpec(memory_space=pltpu.HBM)


def in_hbm(x):
    return pltpu.with_memory_space_constraint(x, pltpu.HBM)


def call(kernel, name, ins, outs, scratch=(), out_space=VMEM, vmem=VMEM_BYTES, aliases=None):
    return pl.pallas_call(
        kernel,
        in_specs=ins,
        out_specs=[out_space] * len(outs),
        out_shape=[jax.ShapeDtypeStruct(shape, kind) for shape, kind in outs],
        scratch_shapes=list(scratch),
        input_output_aliases=aliases or {},
        compiler_params=pltpu.CompilerParams(vmem_limit_bytes=vmem),
        name=name,
    )


def shards(groups, owners, operators, counts, pair_rows, gap):
    slots, h, cases = gap.shape[2:]
    width = cases // PARTS
    evens, odds = pairings(groups, owners)
    forward = [(s, (s + 1) % owners) for s in range(owners)]
    backward = [(t, s) for s, t in forward]
    field = ((slots, cases, h), F32)
    inner = ((slots - 1, cases, h), F32)
    block = ((cases, h), F32)
    part = ((width, h), F32)
    matrices = ((slots - 1, 2 * h, h), BF16)
    pair = ((4 * h, h), BF16)

    def exchange(even, odd):
        odd = lax.ppermute(odd, ("grp", "sub"), odds)
        even = lax.ppermute(even, ("grp", "sub"), evens)
        return even, odd

    gap = in_hbm(gap)
    ends, marks, pairs = call(
        functools.partial(first_kernel, owners),
        "first_ends",
        [SMEM, HBM, HBM, HBM],
        [block, ((slots + 4, 8, h), F32), ((slots, h), jnp.int32)],
        [pltpu.VMEM((h, cases), F32), pltpu.SemaphoreType.DMA((2,))],
        vmem=FIRST_VMEM_BYTES,
    )(counts, operators, in_hbm(pair_rows), gap)
    before = lax.ppermute(ends, "sub", forward)
    own, lower, upper, even_operator, odd_operator, residual, direction, *beside = call(
        operator_kernel,
        "block_operators",
        [SMEM, VMEM, VMEM, VMEM, HBM],
        [matrices] * 3 + [pair] * 2 + [inner] * 2 + [block] * 2,
        [pltpu.VMEM((slots - 1, h, cases), F32), pltpu.SemaphoreType.DMA],
    )(counts, operators, pairs, marks, gap)
    got = call(
        functools.partial(first_edge_kernel, slots, PARTS), "first_edges", [VMEM] * 7, [part] * (6 * PARTS)
    )(even_operator, odd_operator, marks, ends, before, *beside)
    states = [got[6 * k : 6 * k + 6] for k in range(PARTS)]
    total = jnp.zeros(field[0], F32)
    for step, factors in enumerate(chebyshev_factors() + [None]):
        if factors is None:
            came = [lax.ppermute(state[4], "sub", backward) for state in states]
        else:
            came = [exchange(state[4], state[5]) for state in states]
        outs = [inner, field, inner, block, block]
        if factors is None:
            outs = [(gap.shape, F32)] * 2
        turned = pltpu.VMEM((slots, h, cases), F32)
        got = call(
            functools.partial(inner_kernel, factors, PARTS),
            "inner_blocks",
            [VMEM] * (7 + 2 * PARTS),
            outs,
            [turned, turned, pltpu.SemaphoreType.DMA((2, slots))] if factors is None else [],
            HBM if factors is None else VMEM,
        )(own, lower, upper, marks, direction, residual, *(s[2] for s in states), *(s[3] for s in states), total)
        residual, total = got[:2]
        if factors is not None:
            direction, *beside = got[2:]
            states = [
                call(
                    functools.partial(edge_kernel, factors, slots, k * width, step == ITERS - 2),
                    "edge_blocks",
                    [VMEM] * 13,
                    [part] * (5 if step == ITERS - 2 else 6),
                )(even_operator, odd_operator, marks, *beside, *states[k], *came[k])
                for k in range(PARTS)
            ]
    (residual,) = call(
        functools.partial(last_kernel, PARTS, slots),
        "last_residual",
        [SMEM, VMEM, HBM] + [VMEM] * (3 * PARTS),
        [(gap.shape, F32)],
        [pltpu.VMEM((h, cases), F32), pltpu.SemaphoreType.DMA],
        HBM,
        aliases={2: 0},
    )(counts, marks, residual, *(s[n] for n in (0, 1) for s in states), *came)
    return total, residual


def solution(mesh):
    groups, owners = mesh.shape["grp"], mesh.shape["sub"]
    return jax.shard_map(
        functools.partial(shards, groups, owners),
        mesh=mesh,
        in_specs=(
            P("grp", "sub", None, None, None),
            P("grp", "sub"),
            P("grp", "sub", None, None),
            P("grp", "sub", None, None, None),
        ),
        out_specs=(P("grp", "sub", None, None, None), P("grp", "sub", None, None, None)),
        check_vma=False,
    )
```

```python
import functools

import jax
import jax.numpy as jnp
from jax import lax
from jax.experimental import pallas as pl
from jax.experimental.pallas import tpu as pltpu
from jax.sharding import PartitionSpec as P

ITERS = 6
LOWER = 1.0
UPPER = 14.0
CENTRE = (UPPER + LOWER) / 2.0
RADIUS = (UPPER - LOWER) / 2.0
BF16 = jnp.bfloat16
F32 = jnp.float32
PARTS = 2
VMEM_BYTES = 24 * 1024 * 1024
FIRST_VMEM_BYTES = 52 * 1024 * 1024


def chebyshev_factors():
    spread = CENTRE / RADIUS
    rho = 1.0 / spread
    factors = []
    for _ in range(ITERS - 1):
        rho_new = 1.0 / (2.0 * spread - rho)
        factors.append((rho_new * rho, 2.0 * rho_new / RADIUS))
        rho = rho_new
    return factors


def pairings(groups, owners):
    found = []
    for first in (0, 1):
        route = []
        for g in range(groups):
            for s in range(owners):
                t = s + 1 if (s - first) % 2 == 0 else s - 1
                h = g
                if t < 0 or t >= owners:
                    t = s
                    h = g ^ 1
                if h < groups:
                    route.append((g * owners + s, h * owners + t))
        found.append(route)
    return found


def halves(x):
    high = x.astype(BF16)
    return high, (x - high.astype(F32)).astype(BF16)


def operand(x):
    high, low = halves(x)
    return jnp.concatenate([high, low], axis=0), high


def split_dot(cases, matrix):
    both, high = cases
    h = matrix.shape[0] // 2
    tall = jnp.dot(both, matrix[:h], preferred_element_type=F32)
    rows = high.shape[0]
    return tall[:rows] + tall[rows:] + jnp.dot(high, matrix[h:], preferred_element_type=F32)


def beside(x, y):
    return tuple(jnp.concatenate(pair, axis=1) for pair in zip(x, y))


def dot_nt(a, b):
    return lax.dot_general(a, b, (((1,), (1,)), ((), ())), preferred_element_type=F32)


def signed_placement(pairs, scale):
    h = pairs.shape[1]
    rows = lax.broadcasted_iota(jnp.int32, (h, h), 0)
    return jnp.where(rows == jnp.abs(pairs) - 1, jnp.where(pairs > 0, scale, -scale), 0.0).astype(BF16)


def row(marks, k):
    return marks[k, pl.ds(0, 1), :]


def mark_places(slots):
    return dict(even=slots, alone=slots + 1, evens=slots + 2, odds=slots + 3)


def first_kernel(owners, counts, operators, pairs, gap, ends, marks, pairs_out, source, sems):
    slots = pairs_out.shape[0]
    count = counts[0, 0]
    copies = [
        pltpu.make_async_copy(gap.at[0, 0, count - 1], source, sems.at[0]),
        pltpu.make_async_copy(pairs.at[0, 0], pairs_out, sems.at[1]),
    ]
    for copy in copies:
        copy.start()
    pos = lax.axis_index("sub")
    is_even = lax.rem(pos, 2) == 0
    place = mark_places(slots)
    has_left, has_right = pos > 0, pos < owners - 1
    flags = [count - 1 == j for j in range(slots)] + [None] * 4
    flags[place["even"]] = is_even
    flags[place["alone"]] = count == 1
    flags[place["evens"]] = jnp.logical_or(jnp.logical_and(is_even, has_right), jnp.logical_and(~is_even, has_left))
    flags[place["odds"]] = jnp.logical_or(jnp.logical_and(is_even, has_left), jnp.logical_and(~is_even, has_right))
    for k, flag in enumerate(flags):
        marks[k] = jnp.full(marks.shape[1:], jnp.where(flag, 1.0, 0.0), F32)
    copies[0].wait()
    ends[...] = source[...].T * jnp.where(has_right, 1.0, 0.0)
    copies[1].wait()


def put_beside(marks, slots, blocks, beside_even, beside_odd):
    is_even = row(marks, mark_places(slots)["even"]) > 0.5
    first, before_last = blocks[0], sum(row(marks, j + 1) * blocks[j] for j in range(slots - 1))
    beside_even[...] = jnp.where(is_even, before_last, first)
    beside_odd[...] = jnp.where(is_even, first, before_last)


def operator_kernel(counts, operators, pairs, marks, gap, own_out, lower_out, upper_out, even_out, odd_out, residual, direction, beside_even, beside_odd, source, sem):
    slots, h = pairs.shape
    count = counts[0, 0]
    copy = pltpu.make_async_copy(gap.at[0, 0, pl.ds(0, slots - 1)], source, sem)
    copy.start()
    is_even = lax.rem(lax.axis_index("sub"), 2) == 0
    low = pl.ds(h, h)
    for j in range(slots):
        row_pairs = pairs[pl.ds(j, 1), :]
        place = signed_placement(row_pairs, 1.0)
        parts = halves(operators[0, 0, j])
        placed = [jnp.dot(place, part[:h], preferred_element_type=F32) for part in parts]
        uppers = [(-part[:, h:]).T.astype(BF16) for part in placed]
        placed = [part[:, :h].astype(BF16) for part in placed]
        if j > 0:
            live = jnp.where(j < count, 1.0, 0.0)
            scaled = signed_placement(row_pairs, live)
            square = dot_nt(jnp.concatenate([scaled, scaled], axis=1), jnp.concatenate(placed, axis=1))
            put_halves(own_out, j - 1, square + operators[0, 0, j - 1, low, low].T * live)
            upper_out[j - 1, pl.ds(0, h), :], upper_out[j - 1, low, :] = uppers
        if j < slots - 1:
            scaled = signed_placement(row_pairs, jnp.where(j < count - 1, -1.0, 0.0))
            for k, part in enumerate(parts):
                lower_out[j, pl.ds(k * h, h), :] = dot_nt(scaled, part[h:, :h]).astype(BF16)

        def put_first(out, place=place, placed=placed, uppers=uppers):
            for k in range(2):
                out[pl.ds(2 * k * h, h), :] = dot_nt(place, placed[k]).astype(BF16)
                out[pl.ds((2 * k + 1) * h, h), :] = uppers[k]

        def put_last(out, j=j, row_pairs=row_pairs, parts=parts):
            out[pl.ds(0, h), :], out[pl.ds(2 * h, h), :] = halves(operators[0, 0, j, low, low].T)
            turned = signed_placement(row_pairs, -1.0)
            for k, part in enumerate(parts):
                out[pl.ds((2 * k + 1) * h, h), :] = dot_nt(turned, part[h:, :h]).astype(BF16)

        if j == 0:
            pl.when(is_even)(functools.partial(put_first, odd_out))
            pl.when(~is_even)(functools.partial(put_first, even_out))
        is_last = count - 1 == j
        pl.when(jnp.logical_and(is_last, is_even))(functools.partial(put_last, even_out))
        pl.when(jnp.logical_and(is_last, ~is_even))(functools.partial(put_last, odd_out))
    copy.wait()
    for j in range(slots - 1):
        residual[j] = source[j].T * jnp.where(j < count - 1, 1.0, 0.0)
        direction[j] = residual[j] / CENTRE
    put_beside(marks, slots, [direction[j] for j in range(slots - 1)], beside_even, beside_odd)


def put_halves(out, j, matrix):
    h = matrix.shape[0]
    out[j, pl.ds(0, h), :], out[j, pl.ds(h, h), :] = halves(matrix)


def give(marks, slots, even, odd, beside_even, beside_odd, even_operator, odd_operator):
    alone = row(marks, mark_places(slots)["alone"]) > 0.5
    next_even, next_odd = jnp.where(alone, odd, beside_even), jnp.where(alone, even, beside_odd)
    return (
        split_dot(beside(operand(even), operand(next_even)), even_operator[...]),
        split_dot(beside(operand(odd), operand(next_odd)), odd_operator[...]),
    )


def first_edge_kernel(slots, start, even_operator, odd_operator, marks, ends, before, beside_even, beside_odd, *outs):
    place = mark_places(slots)
    rows = pl.ds(start, outs[0].shape[0])
    is_even = row(marks, place["even"]) > 0.5
    last, first = ends[rows, :], before[rows, :]
    even = jnp.where(is_even, last, first) * row(marks, place["evens"])
    odd = jnp.where(is_even, first, last) * row(marks, place["odds"])
    directions = even / CENTRE, odd / CENTRE
    given = give(marks, slots, *directions, beside_even[rows, :], beside_odd[rows, :], even_operator, odd_operator)
    for out, x in zip(outs, (even, odd, *directions, *given)):
        out[...] = x


def edge_kernel(factors, slots, start, ends, even_operator, odd_operator, marks, beside_even, beside_odd, *refs):
    even_r, odd_r, even_v, odd_v, even_sent, odd_sent, even_in, odd_in = (ref[...] for ref in refs[:8])
    outs = refs[8:]
    place = mark_places(slots)
    rows = pl.ds(start, even_r.shape[0])
    even_r = (even_r - (even_sent + even_in)) * row(marks, place["evens"])
    odd_r = (odd_r - (odd_sent + odd_in)) * row(marks, place["odds"])
    even_v = factors[0] * even_v + factors[1] * even_r
    odd_v = factors[0] * odd_v + factors[1] * odd_r
    given = give(marks, slots, even_v, odd_v, beside_even[rows, :], beside_odd[rows, :], even_operator, odd_operator)
    if ends:
        is_even = row(marks, place["even"]) > 0.5
        last_r, last_given = jnp.where(is_even, even_r, odd_r), jnp.where(is_even, given[0], given[1])
        results = last_r, last_given, even_v, odd_v, jnp.where(is_even, given[1], given[0])
    else:
        results = even_r, odd_r, even_v, odd_v, *given
    for out, x in zip(outs, results):
        out[...] = x


def inner_kernel(factors, parts, own, lower, upper, marks, direction, residual, *rest):
    inner = residual.shape[0]
    slots = inner + 1
    even = jnp.concatenate([ref[...] for ref in rest[:parts]], axis=0)
    odd = jnp.concatenate([ref[...] for ref in rest[parts : 2 * parts]], axis=0)
    total, *outs = rest[2 * parts :]
    is_even = row(marks, mark_places(slots)["even"]) > 0.5
    last, before = jnp.where(is_even, even, odd), jnp.where(is_even, odd, even)
    blocks = [row(marks, j) * last + (direction[j] if j < inner else 0.0) for j in range(slots)]
    cases = [operand(block) for block in blocks]
    if factors is None:
        residual_out, total_out, residual_ready, total_ready, sems = outs
        pairs = ((total_ready, total_out), (residual_ready, residual_out))
        copies = [[pltpu.make_async_copy(x.at[j], y.at[0, 0, j], sems.at[n, j]) for j in range(slots)] for n, (x, y) in enumerate(pairs)]
    else:
        residual_out, total_out = outs[:2]
    for j in range(slots):
        summed = total[j] + blocks[j]
        if factors is None:
            total_ready[j] = summed.T
            copies[0][j].start()
        else:
            total_out[j] = summed
    nexts = []
    for j in range(inner):
        image = split_dot(cases[j], own[j]) + split_dot(cases[j + 1], upper[j])
        image += split_dot(cases[j - 1] if j > 0 else operand(before), lower[j])
        left_over = residual[j] - image
        if factors is None:
            residual_ready[j] = left_over.T
            copies[1][j].start()
            continue
        residual_out[j] = left_over
        nexts.append(factors[0] * direction[j] + factors[1] * left_over)
        outs[2][j] = nexts[j]
    if factors is not None:
        put_beside(marks, slots, nexts, outs[3], outs[4])
    else:
        residual_ready[inner] = jnp.zeros(residual_ready.shape[1:], F32)
        copies[1][inner].start()
        for copy in copies[0] + copies[1]:
            copy.wait()


def last_kernel(parts, slots, counts, marks, _, *refs):
    out, ready, sem = refs[3 * parts :]
    place = mark_places(slots)
    last_r, last_given, came = (
        jnp.concatenate([ref[...] for ref in refs[n * parts : (n + 1) * parts]], axis=0) for n in range(3)
    )
    is_even = row(marks, place["even"]) > 0.5
    shared = jnp.where(is_even, row(marks, place["evens"]), row(marks, place["odds"]))
    ready[...] = ((last_r - (last_given + came)) * shared).T
    copy = pltpu.make_async_copy(ready, out.at[0, 0, counts[0, 0] - 1], sem)
    copy.start()
    copy.wait()


VMEM = pl.BlockSpec(memory_space=pltpu.VMEM)
SMEM = pl.BlockSpec(memory_space=pltpu.SMEM)
HBM = pl.BlockSpec(memory_space=pltpu.HBM)


def in_hbm(x):
    return pltpu.with_memory_space_constraint(x, pltpu.HBM)


def call(kernel, name, ins, outs, scratch=(), out_space=VMEM, vmem=VMEM_BYTES, aliases=None):
    return pl.pallas_call(
        kernel,
        in_specs=ins,
        out_specs=[out_space] * len(outs),
        out_shape=[jax.ShapeDtypeStruct(shape, kind) for shape, kind in outs],
        scratch_shapes=list(scratch),
        input_output_aliases=aliases or {},
        compiler_params=pltpu.CompilerParams(vmem_limit_bytes=vmem),
        name=name,
    )


def shards(groups, owners, operators, counts, pair_rows, gap):
    slots, h, cases = gap.shape[2:]
    width = cases // PARTS
    evens, odds = pairings(groups, owners)
    forward = [(s, (s + 1) % owners) for s in range(owners)]
    backward = [(t, s) for s, t in forward]
    field = ((slots, cases, h), F32)
    inner = ((slots - 1, cases, h), F32)
    block = ((cases, h), F32)
    part = ((width, h), F32)
    matrices = ((slots - 1, 2 * h, h), BF16)
    pair = ((4 * h, h), BF16)

    def exchange(even, odd):
        odd = lax.ppermute(odd, ("grp", "sub"), odds)
        even = lax.ppermute(even, ("grp", "sub"), evens)
        return even, odd

    gap = in_hbm(gap)
    ends, marks, pairs = call(
        functools.partial(first_kernel, owners),
        "first_ends",
        [SMEM, HBM, HBM, HBM],
        [block, ((slots + 4, 8, h), F32), ((slots, h), jnp.int32)],
        [pltpu.VMEM((h, cases), F32), pltpu.SemaphoreType.DMA((2,))],
        vmem=FIRST_VMEM_BYTES,
    )(counts, operators, in_hbm(pair_rows), gap)
    before = lax.ppermute(ends, "sub", forward)
    own, lower, upper, even_operator, odd_operator, residual, direction, *beside = call(
        operator_kernel,
        "block_operators",
        [SMEM, VMEM, VMEM, VMEM, HBM],
        [matrices] * 3 + [pair] * 2 + [inner] * 2 + [block] * 2,
        [pltpu.VMEM((slots - 1, h, cases), F32), pltpu.SemaphoreType.DMA],
    )(counts, operators, pairs, marks, gap)
    states = [
        call(functools.partial(first_edge_kernel, slots, k * width), "first_edges", [VMEM] * 7, [part] * 6)(
            even_operator, odd_operator, marks, ends, before, *beside
        )
        for k in range(PARTS)
    ]
    total = jnp.zeros(field[0], F32)
    for step, factors in enumerate(chebyshev_factors() + [None]):
        if factors is None:
            came = [lax.ppermute(state[4], "sub", backward) for state in states]
        else:
            came = [exchange(state[4], state[5]) for state in states]
        outs = [inner, field, inner, block, block]
        if factors is None:
            outs = [(gap.shape, F32)] * 2
        turned = pltpu.VMEM((slots, h, cases), F32)
        got = call(
            functools.partial(inner_kernel, factors, PARTS),
            "inner_blocks",
            [VMEM] * (7 + 2 * PARTS),
            outs,
            [turned, turned, pltpu.SemaphoreType.DMA((2, slots))] if factors is None else [],
            HBM if factors is None else VMEM,
        )(own, lower, upper, marks, direction, residual, *(s[2] for s in states), *(s[3] for s in states), total)
        residual, total = got[:2]
        if factors is not None:
            direction, *beside = got[2:]
            states = [
                call(
                    functools.partial(edge_kernel, factors, slots, k * width, step == ITERS - 2),
                    "edge_blocks",
                    [VMEM] * 13,
                    [part] * (5 if step == ITERS - 2 else 6),
                )(even_operator, odd_operator, marks, *beside, *states[k], *came[k])
                for k in range(PARTS)
            ]
    (residual,) = call(
        functools.partial(last_kernel, PARTS, slots),
        "last_residual",
        [SMEM, VMEM, HBM] + [VMEM] * (3 * PARTS),
        [(gap.shape, F32)],
        [pltpu.VMEM((h, cases), F32), pltpu.SemaphoreType.DMA],
        HBM,
        aliases={2: 0},
    )(counts, marks, residual, *(s[n] for n in (0, 1) for s in states), *came)
    return total, residual


def solution(mesh):
    groups, owners = mesh.shape["grp"], mesh.shape["sub"]
    return jax.shard_map(
        functools.partial(shards, groups, owners),
        mesh=mesh,
        in_specs=(
            P("grp", "sub", None, None, None),
            P("grp", "sub"),
            P("grp", "sub", None, None),
            P("grp", "sub", None, None, None),
        ),
        out_specs=(P("grp", "sub", None, None, None), P("grp", "sub", None, None, None)),
        check_vma=False,
    )
```
